256 devices in a mesh: seq: 8 (over y, core), dp: 32 (over z, x).
Axes of the slice: x: 4, y: 4, z: 8, core: 2. Of those that a mesh axis runs over, the one named last changes fastest.
Arguments:
- q_rows: bfloat16 [32768, 2048], P(('seq', 'dp')), may hold values from -6 to 6
- key_rows: bfloat16 [32768, 512], P(('seq', 'dp')), may hold values from -6 to 6
- value_rows: bfloat16 [32768, 512], P(('seq', 'dp')), may hold values from -6 to 6
- pack_peer: int32 [4096], P(('seq', 'dp')), may hold values from 0 to 31, as said below
- pack_slot: int32 [4096], P(('seq', 'dp')), may hold values from 0 to 15
- doc_ids: int32 [32, 1024], P('dp'), may hold values from 0 to 7, never falling along the last dimension, each value on 1 to 512 neighbouring positions
- grad_out: bfloat16 [32, 1024, 2048], P('dp', 'seq'), may hold values from -6 to 6
- out_weight: bfloat16 [2048, 2048], P(('seq', 'dp')), may hold values from -0.125 to 0.125
Outputs:
- dq_rows: bfloat16 [32768, 2048], P(('seq', 'dp'))
- key_gradient_rows: bfloat16 [32768, 512], P(('seq', 'dp'))
- value_gradient_rows: bfloat16 [32768, 512], P(('seq', 'dp'))
- wo_grad: float32 [2048, 2048], P(('seq', 'dp'))
The draws below stay inside these ranges and needn't reach their ends.
Inputs may be any that keep to these rules, and one draw needn't show every extreme that they name: `pack_peer`: blocks keep their seq index; every block position of every packed sequence receives exactly one block; the 16 blocks of one device send at most 1 block to one packed sequence, and exactly 1 to some.
All inputs are finite; a program needn't handle non-finite values.
Results may differ from the reference program's by a relative error of at most 0.03.
Values may be sent and summed in bfloat16 or wider, within the bound.
A program may use at most 64 MiB of HBM per device.

```python
import math
import jax
import jax.numpy as jnp
import numpy as np
from jax import lax

QUERY_HEADS = 16
KEY_VALUE_HEADS = 4
HEAD_SIZE = 128
D = 2048
T_DEV = 128
NB = 16
PACK = 8
DOCS = 8
GROUP_QUERY_HEADS = 2
SEQUENCE_LENGTH = 1024
SAMPLE_ROWS = 32768
N_SEQ = 8
N_DP = 32


def pack_tables(key):
    base = jax.random.fold_in(key, 11)
    seq_keys = jax.random.split(jax.random.fold_in(base, 1), N_SEQ)
    shifts = jax.vmap(lambda single: jax.random.permutation(single, N_DP))(seq_keys)
    slot_keys = jax.random.split(jax.random.fold_in(base, 2), N_SEQ * N_DP)
    slots = jax.vmap(lambda single: jax.random.permutation(single, NB))(slot_keys).reshape(N_SEQ, N_DP, NB)
    order_keys = jax.random.split(jax.random.fold_in(base, 3), N_SEQ * N_DP)
    order = jax.vmap(lambda single: jax.random.permutation(single, NB))(order_keys).reshape(N_SEQ, N_DP, NB)
    seq_index = jnp.arange(N_SEQ, dtype=jnp.int32)[:, None, None]
    source = jnp.arange(N_DP, dtype=jnp.int32)[None, :, None]
    shift = shifts[seq_index, order % N_DP]
    target = (source + shift) % N_DP
    landing = slots[seq_index, target, order]
    return (target.reshape(-1).astype(jnp.int32), landing.reshape(-1).astype(jnp.int32))


def draw_pack_peer(key, part):
    return pack_tables(key)[0]


def draw_pack_slot(key, part):
    return pack_tables(key)[1]


def draw_q_rows(key, part):
    value_entries = jnp.clip(jax.random.normal(jax.random.fold_in(key, 1), (SAMPLE_ROWS, D), jnp.float32), -6.0, 6.0)
    return value_entries.astype(jnp.bfloat16)


def draw_key_rows(key, part):
    value_entries = jnp.clip(jax.random.normal(jax.random.fold_in(key, 21), (SAMPLE_ROWS, KEY_VALUE_HEADS * HEAD_SIZE), jnp.float32), -6.0, 6.0)
    return value_entries.astype(jnp.bfloat16)


def block_scale(rng, extent, cuts, smallest, largest):
    def one(position, shards_of):
        draws = jax.random.uniform(jax.random.fold_in(jax.random.fold_in(rng, 6), position), (shards_of,), jnp.float32, smallest / len(cuts), largest / len(cuts))
        return jnp.repeat(jnp.exp(draws), extent[position] // shards_of).reshape((-1,) + (1,) * (len(extent) - position - 1))

    gain = one(*cuts[0])
    for cut in cuts[1:]:
        gain = gain * one(*cut)
    return gain


def split_up(amount, total, reach, skew):
    portions = [(1 << 20) // math.isqrt(standing ** skew) + 1 for standing in range(2, amount + 1)]
    rest, counts = total - reach - (amount - 1), [1] * (amount - 1)
    while rest > 0:
        candidates = [i for i in range(amount - 1) if counts[i] < reach]
        mass, budget = sum([portions[i] for i in candidates]), rest
        for i in candidates:
            extra = min(reach - counts[i], max(1, budget * portions[i] // mass), rest)
            counts[i] = counts[i] + extra
            rest = rest - extra
    return np.array([reach] + counts)


def ragged(own_key, number_of, total, bound, skew):
    if number_of == 2:
        one = jax.random.randint(own_key, (), max(1, total - bound), min(bound, total - 1) + 1)
        return jnp.stack([one, total - one])
    lengths = jnp.asarray(split_up(number_of, total, bound, skew), jnp.int32)
    couples = (number_of - 1) // 2
    source_of, taker = lengths[1:1 + 2 * couples:2], lengths[2:2 + 2 * couples:2]
    room = jnp.minimum(source_of - 1, bound - taker)
    shifted = jax.random.randint(jax.random.fold_in(own_key, 1), (couples,), 0, 1 << 20) % (room + 1)
    lengths = lengths.at[1:1 + 2 * couples:2].set(source_of - shifted).at[2:2 + 2 * couples:2].set(taker + shifted)
    return lengths[jax.random.permutation(jax.random.fold_in(own_key, 2), number_of)]


def noise(key, extent, spread, most, pieces=(), kind=jnp.bfloat16):
    result = spread * jax.random.normal(key, extent, jnp.float32)
    if pieces:
        result = result * block_scale(key, extent, pieces, -0.22, 0.18)
    return jnp.clip(result, -most, most).astype(kind)


def setup_inputs(seed: int = 0) -> dict:
    seeds = jax.random.split(jax.random.key(seed), 9)
    return {
        "q_rows": draw_q_rows(jax.random.fold_in(seeds[8], 71), 0),
        "key_rows": draw_key_rows(jax.random.fold_in(seeds[8], 71), 0),
        "value_rows": noise(seeds[2], (SAMPLE_ROWS, KEY_VALUE_HEADS * HEAD_SIZE), 1.0, 6.0, ((0, 256),)),
        "pack_peer": draw_pack_peer(jax.random.fold_in(seeds[8], 71), 0),
        "pack_slot": draw_pack_slot(jax.random.fold_in(seeds[8], 71), 0),
        "doc_ids": jax.vmap(lambda own: jnp.searchsorted(jnp.cumsum(ragged(own, DOCS, SEQUENCE_LENGTH, SEQUENCE_LENGTH // 2, 2)), jnp.arange(SEQUENCE_LENGTH), side="right"))(jax.random.split(seeds[5], N_DP)).reshape((N_DP, SEQUENCE_LENGTH)).astype(jnp.int32),
        "grad_out": noise(seeds[6], (N_DP, SEQUENCE_LENGTH, D), 1.0, 6.0, ((0, 32), (1, 8))),
        "out_weight": noise(seeds[7], (D, D), D ** -0.5, 0.125, ((0, 256),)),
    }


NEG_FILL = -1e+30

def pack_positions(pack_peer, pack_slot):
    block_index = jnp.arange(N_SEQ * N_DP * NB, dtype=jnp.int32)
    shard_seq = block_index // (N_DP * NB)
    first_row = pack_peer * SEQUENCE_LENGTH + shard_seq * T_DEV + pack_slot * PACK
    offsets = jnp.arange(PACK, dtype=jnp.int32)
    return (first_row[:, None] + offsets[None, :]).reshape(-1).astype(jnp.int32)

def head_pass(query, key_part, value_part, grad_part, allowed, soft_scale):
    raw = jnp.dot(query, key_part.T, preferred_element_type=jnp.float32) * soft_scale
    masked = jnp.where(allowed, raw, NEG_FILL)
    peak = lax.optimization_barrier(jnp.max(masked, axis=1, keepdims=True))
    total = lax.optimization_barrier(jnp.sum(jnp.where(allowed, jnp.exp(masked - peak), 0.0), axis=1, keepdims=True))
    log_total = peak + jnp.log(total)
    weights = jnp.where(allowed, jnp.exp(masked - log_total), 0.0)
    weights_low = weights.astype(jnp.bfloat16)
    attended = jnp.dot(weights_low, value_part, preferred_element_type=jnp.float32).astype(jnp.bfloat16)
    delta = lax.optimization_barrier(jnp.sum(grad_part.astype(jnp.float32) * attended.astype(jnp.float32), axis=1, keepdims=True))
    dweights = jnp.dot(grad_part, value_part.T, preferred_element_type=jnp.float32)
    dscores = (weights * (dweights - delta)).astype(jnp.bfloat16)
    dquery = (jnp.dot(dscores, key_part, preferred_element_type=jnp.float32) * soft_scale).astype(jnp.bfloat16)
    dkey = jnp.dot(dscores.T, query, preferred_element_type=jnp.float32)
    dvalue = jnp.dot(weights_low.T, grad_part, preferred_element_type=jnp.float32)
    return (attended, dquery, dkey, dvalue)

def group_heads(per_head, factor):
    head_grouped = lax.optimization_barrier(jnp.sum(per_head.reshape(QUERY_HEADS // GROUP_QUERY_HEADS, GROUP_QUERY_HEADS, SEQUENCE_LENGTH, HEAD_SIZE), axis=1)) * factor
    head_grouped = lax.optimization_barrier(head_grouped.astype(jnp.bfloat16)).astype(jnp.float32)
    combined_heads = lax.optimization_barrier(jnp.sum(head_grouped.reshape(KEY_VALUE_HEADS, QUERY_HEADS // KEY_VALUE_HEADS // GROUP_QUERY_HEADS, SEQUENCE_LENGTH, HEAD_SIZE), axis=1)).astype(jnp.bfloat16)
    return jnp.transpose(combined_heads, (1, 0, 2)).reshape(SEQUENCE_LENGTH, KEY_VALUE_HEADS * HEAD_SIZE)

def reference(q_rows, key_rows, value_rows, pack_peer, pack_slot, doc_ids, grad_out, out_weight):
    soft_scale = 1.0 / math.sqrt(HEAD_SIZE)
    token_places = pack_positions(pack_peer, pack_slot)
    packed_q = jnp.zeros((N_DP * SEQUENCE_LENGTH, D), jnp.bfloat16).at[token_places].set(q_rows).reshape(N_DP, SEQUENCE_LENGTH, D)
    packed_keys = jnp.zeros((N_DP * SEQUENCE_LENGTH, KEY_VALUE_HEADS * HEAD_SIZE), jnp.bfloat16).at[token_places].set(key_rows).reshape(N_DP, SEQUENCE_LENGTH, KEY_VALUE_HEADS * HEAD_SIZE)
    packed_values = jnp.zeros((N_DP * SEQUENCE_LENGTH, KEY_VALUE_HEADS * HEAD_SIZE), jnp.bfloat16).at[token_places].set(value_rows).reshape(N_DP, SEQUENCE_LENGTH, KEY_VALUE_HEADS * HEAD_SIZE)
    token_pos = jnp.arange(SEQUENCE_LENGTH, dtype=jnp.int32)

    def sequence_pass(carry, inputs):
        query_all, key_all, value_all, grad_rows, doc_row = inputs
        allowed = (doc_row[:, None] == doc_row[None, :]) & (token_pos[:, None] >= token_pos[None, :])
        attn_grad = jnp.dot(grad_rows, out_weight.T, preferred_element_type=jnp.float32).astype(jnp.bfloat16)

        def one_head(head_number):
            key_value_head = head_number // (QUERY_HEADS // KEY_VALUE_HEADS)
            query = lax.dynamic_slice_in_dim(query_all, head_number * HEAD_SIZE, HEAD_SIZE, 1)
            key_part = lax.dynamic_slice_in_dim(key_all, key_value_head * HEAD_SIZE, HEAD_SIZE, 1)
            value_part = lax.dynamic_slice_in_dim(value_all, key_value_head * HEAD_SIZE, HEAD_SIZE, 1)
            grad_part = lax.dynamic_slice_in_dim(attn_grad, head_number * HEAD_SIZE, HEAD_SIZE, 1)
            return head_pass(query, key_part, value_part, grad_part, allowed, soft_scale)
        attended, dquery, dkey, dvalue = lax.map(one_head, jnp.arange(QUERY_HEADS, dtype=jnp.int32))
        attn = jnp.transpose(attended, (1, 0, 2)).reshape(SEQUENCE_LENGTH, D)
        dq_seq = jnp.transpose(dquery, (1, 0, 2)).reshape(SEQUENCE_LENGTH, D)
        dk_seq = group_heads(dkey, soft_scale)
        dv_seq = group_heads(dvalue, 1.0)
        shard_out = attn.reshape(N_SEQ, T_DEV, D).astype(jnp.float32)
        shard_grad = grad_rows.reshape(N_SEQ, T_DEV, D).astype(jnp.float32)
        partials = jnp.einsum('std,ste->sde', shard_out, shard_grad)
        partials = lax.optimization_barrier(partials.astype(jnp.bfloat16)).astype(jnp.float32)
        carry = carry + lax.optimization_barrier(jnp.sum(partials, axis=0))
        return (carry, (dq_seq, dk_seq, dv_seq))
    start_grad = jnp.zeros((D, D), jnp.float32)
    summed, (dq_packed, key_gradient_packed, value_gradient_packed) = lax.scan(sequence_pass, start_grad, (packed_q, packed_keys, packed_values, grad_out, doc_ids))
    wo_grad = summed * (8.0 / math.sqrt(N_DP * SEQUENCE_LENGTH))
    dq_rows = dq_packed.reshape(N_DP * SEQUENCE_LENGTH, D)[token_places]
    key_gradient_rows = key_gradient_packed.reshape(N_DP * SEQUENCE_LENGTH, KEY_VALUE_HEADS * HEAD_SIZE)[token_places]
    value_gradient_rows = value_gradient_packed.reshape(N_DP * SEQUENCE_LENGTH, KEY_VALUE_HEADS * HEAD_SIZE)[token_places]
    return (dq_rows, key_gradient_rows, value_gradient_rows, wo_grad)
```

```python
import math

import jax
import jax.numpy as jnp
from jax import lax
from jax.experimental import pallas as pl
from jax.experimental.pallas import tpu as pltpu
from jax.sharding import PartitionSpec as P

HEAD = 128
PACK = 8
NEG_FILL = -1e30
MESH = pl.DeviceIdType.MESH
BF16 = jnp.bfloat16
F32 = jnp.float32
N_SEQ, N_Y = 8, 4
N_DP, N_Z, N_X = 32, 8, 4
TOK = 128
SEQ_LEN = 1024
D = 2048
KV_COLS = 1024
QB = 256
SOFT_SCALE = 1.0 / math.sqrt(HEAD)
GRAD_SCALE = 8.0 / math.sqrt(N_DP * SEQ_LEN)
VMEM = pl.BlockSpec(memory_space=pltpu.VMEM)


def nn(a, b):
    return lax.dot_general(a, b, (((1,), (0,)), ((), ())), preferred_element_type=F32)


def nt(a, b):
    return lax.dot_general(a, b, (((1,), (1,)), ((), ())), preferred_element_type=F32)


def remote(src, dst, send, recv, seq, dp):
    return pltpu.make_async_remote_copy(
        src_ref=src, dst_ref=dst, send_sem=send, recv_sem=recv, device_id=(seq, dp), device_id_type=MESH
    )


def greet(s, d):
    barrier = pltpu.get_barrier_semaphore()

    def along_dp(i, carry):
        pl.semaphore_signal(barrier, inc=1, device_id=(s, lax.rem(d + i, N_DP)), device_id_type=MESH)
        return carry

    def along_seq(i, carry):
        pl.semaphore_signal(barrier, inc=1, device_id=(lax.rem(s + i, N_SEQ), d), device_id_type=MESH)
        return carry

    lax.fori_loop(1, N_DP, along_dp, 0)
    lax.fori_loop(1, N_SEQ, along_seq, 0)
    return barrier


def wait_greeted(barrier):
    pl.semaphore_wait(barrier, N_DP - 1 + N_SEQ - 1)


def send_slots(slots, came, send, recv, s, d):
    def one(i, carry):
        p = lax.rem(d + i, N_DP)
        remote(slots.at[p], came.at[d], send, recv, s, p).start()
        return carry

    lax.fori_loop(1, N_DP, one, 0)


def wait_bytes(ref, sem):
    pltpu.make_async_copy(ref, ref, sem).wait()


def slot_rows(ref, columns):
    block = ref[:, :, columns]
    return block.astype(F32).reshape(N_DP * PACK, block.shape[2]).astype(BF16)


def as_slots(rows):
    return rows.reshape(N_DP, PACK, rows.shape[1]).astype(BF16)


def forward_exchange(
    q_ref, k_ref, v_ref, target_ref, landing_ref, grad_ref, w_ref,
    q_all, k_all, v_all, came_tag, g_all, w_all,
    slots_t, slots_kv, slots_q, came_kv, came_q, packed_kv, packed_q,
    own, slot_send, slot_recv, head_send, head_recv, g_send, g_recv, w_send, w_recv,
):
    s, d = lax.axis_index("seq"), lax.axis_index("dp")
    y, core = s // 2, lax.rem(s, 2)
    z, x = d // N_X, lax.rem(d, N_X)
    mate = y * 2 + 1 - core
    up, down = lax.rem(y + 1, N_Y) * 2 + core, lax.rem(y + N_Y - 1, N_Y) * 2 + core
    across = lax.rem(y + 2, N_Y) * 2 + core
    barrier = greet(s, d)

    own_g = pltpu.make_async_copy(grad_ref, g_all.at[s], own.at[0])
    own_w = pltpu.make_async_copy(w_ref, w_all.at[z, x], own.at[1])
    own_g.start()
    own_w.start()

    place = (lax.broadcasted_iota(jnp.int32, (N_DP * PACK, TOK), 0) == target_ref[...]).astype(F32).astype(BF16)
    tags = (lax.broadcasted_iota(jnp.int32, (TOK, TOK), 1) == landing_ref[...]).astype(F32).astype(BF16)
    slots_t[...] = as_slots(nn(place, tags))
    for part, ref in enumerate((k_ref, v_ref)):
        for c in range(2):
            cols = slice(part * 512 + c * 256, part * 512 + (c + 1) * 256)
            slots_kv[:, :, cols] = as_slots(nn(place, ref[:, c * 256 : (c + 1) * 256]))
    own_g.wait()
    own_w.wait()
    wait_greeted(barrier)

    g_up = remote(g_all.at[s], g_all.at[s], g_send.at[0], g_recv.at[0], up, d)
    g_down = remote(g_all.at[s], g_all.at[s], g_send.at[1], g_recv.at[1], down, d)
    g_mate = remote(g_all.at[s], g_all.at[s], g_send.at[2], g_recv.at[2], mate, d)
    send_slots(slots_t, came_tag, slot_send.at[0], slot_recv.at[0], s, d)
    g_up.start()
    g_down.start()
    g_mate.start()

    def weight_z(i, carry):
        zz = lax.rem(z + i, N_Z)
        remote(w_all.at[z, x], w_all.at[z, x], w_send.at[0], w_recv.at[0], s, zz * N_X + x).start()
        return carry

    lax.fori_loop(1, N_Z, weight_z, 0)
    send_slots(slots_kv, came_kv, slot_send.at[1], slot_recv.at[1], s, d)

    for g in range(N_SEQ):
        both = nn(place, q_ref[:, g * 256 : (g + 1) * 256])
        slots_q[0, :, :, g * HEAD : (g + 1) * HEAD] = as_slots(both[:, :HEAD])
        slots_q[1, :, :, g * HEAD : (g + 1) * HEAD] = as_slots(both[:, HEAD:])
    for h in range(2):
        send_slots(slots_q.at[h], came_q.at[h], slot_send.at[2 + h], slot_recv.at[2 + h], s, d)

    kept = [
        pltpu.make_async_copy(slots_t.at[d], came_tag.at[d], own.at[0]),
        pltpu.make_async_copy(slots_kv.at[d], came_kv.at[d], own.at[1]),
        pltpu.make_async_copy(slots_q.at[0, d], came_q.at[0, d], own.at[2]),
        pltpu.make_async_copy(slots_q.at[1, d], came_q.at[1, d], own.at[3]),
    ]
    for copy in kept:
        copy.start()
    for copy in kept:
        copy.wait()

    wait_bytes(w_all.at[0 : N_Z - 1, 0], w_recv.at[0])
    wait_bytes(w_all.at[0 : N_Z - 1, 0], w_send.at[0])

    def weight_x(i, carry):
        xx = lax.rem(x + i, N_X)
        remote(w_all.at[:, x], w_all.at[:, x], w_send.at[1], w_recv.at[1], s, z * N_X + xx).start()
        return carry

    lax.fori_loop(1, N_X, weight_x, 0)

    g_up.wait_recv()
    from_down = g_all.at[down]
    half_up = remote(from_down.at[0:64], from_down.at[0:64], g_send.at[3], g_recv.at[3], up, d)
    mate_down = remote(from_down, from_down, g_send.at[4], g_recv.at[4], mate, d)
    half_up.start()
    mate_down.start()
    g_down.wait_recv()
    from_up = g_all.at[up]
    half_down = remote(from_up.at[64:128], from_up.at[64:128], g_send.at[5], g_recv.at[5], down, d)
    mate_up = remote(from_up, from_up, g_send.at[6], g_recv.at[6], mate, d)
    half_down.start()
    mate_up.start()

    wait_bytes(came_tag.at[0 : N_DP - 1], slot_recv.at[0])
    tag_rows = came_tag[...].astype(F32).reshape(N_DP * PACK, TOK)
    gather = tag_rows.T.astype(BF16)
    wait_bytes(came_kv.at[0 : N_DP - 1], slot_recv.at[1])
    for c in range(4):
        two = nn(gather, slot_rows(came_kv, slice(c * 256, (c + 1) * 256))).astype(BF16)
        packed_kv[2 * c] = two[:, :HEAD]
        packed_kv[2 * c + 1] = two[:, HEAD:]

    def keys_out(i, carry):
        t = lax.rem(s + i, N_SEQ)
        remote(packed_kv.at[t // 2], k_all.at[s], head_send.at[0], head_recv.at[0], t, d).start()
        remote(packed_kv.at[4 + t // 2], v_all.at[s], head_send.at[1], head_recv.at[1], t, d).start()
        return carry

    lax.fori_loop(1, N_SEQ, keys_out, 0)
    kept = [
        pltpu.make_async_copy(packed_kv.at[s // 2], k_all.at[s], own.at[0]),
        pltpu.make_async_copy(packed_kv.at[4 + s // 2], v_all.at[s], own.at[1]),
    ]
    for copy in kept:
        copy.start()

    half_up.wait_recv()
    half_down.wait_recv()
    from_across = g_all.at[across]
    mate_across = remote(from_across, from_across, g_send.at[7], g_recv.at[7], mate, d)
    mate_across.start()

    for h in range(2):
        wait_bytes(came_q.at[h, 0 : N_DP - 1], slot_recv.at[2 + h])
        for c in range(4):
            two = nn(gather, slot_rows(came_q.at[h], slice(c * 256, (c + 1) * 256))).astype(BF16)
            packed_q[h, 2 * c] = two[:, :HEAD]
            packed_q[h, 2 * c + 1] = two[:, HEAD:]

        def queries_out(i, carry):
            t = lax.rem(s + i, N_SEQ)
            remote(packed_q.at[h, t], q_all.at[h, s], head_send.at[2 + h], head_recv.at[2 + h], t, d).start()
            return carry

        lax.fori_loop(1, N_SEQ, queries_out, 0)
        keep = pltpu.make_async_copy(packed_q.at[h, s], q_all.at[h, s], own.at[2 + h])
        keep.start()
        kept.append(keep)

    for copy in kept:
        copy.wait()
    for copy in (g_mate, mate_down, mate_up, mate_across):
        copy.wait_recv()
    for copy in (g_up, g_down, g_mate, half_up, mate_down, half_down, mate_up, mate_across):
        copy.wait_send()
    for sem in (w_recv.at[1], w_send.at[1]):
        wait_bytes(w_all.at[:, 0 : N_X - 1], sem)
    wait_bytes(came_tag.at[0 : N_DP - 1], slot_send.at[0])
    wait_bytes(came_kv.at[0 : N_DP - 1], slot_send.at[1])
    for h in range(2):
        wait_bytes(came_q.at[h, 0 : N_DP - 1], slot_send.at[2 + h])
    for sems in (head_recv, head_send):
        wait_bytes(k_all.at[0 : N_SEQ - 1], sems.at[0])
        wait_bytes(v_all.at[0 : N_SEQ - 1], sems.at[1])
        for h in range(2):
            wait_bytes(q_all.at[h, 0 : N_SEQ - 1], sems.at[2 + h])


def attention(q_all, k_ref, v_ref, g_all, w_all, doc_ref, dq_all, dk_ref, dv_ref, wo_ref, g_t, o_t, k_t, v_t, doc_c, dk_sum, dv_sum):
    k_t[...] = k_ref[...].astype(F32).T.astype(BF16)
    v_t[...] = v_ref[...].astype(F32).T.astype(BF16)
    doc_row = doc_ref[...].astype(F32)
    doc_c[...] = jnp.broadcast_to(doc_row, (HEAD, SEQ_LEN)).T
    weight = w_all[...].astype(F32).reshape(2 * HEAD, D).astype(BF16)
    for i in range(SEQ_LEN // QB):
        g_t[:, i * QB : (i + 1) * QB] = nt(weight, g_all[i * QB : (i + 1) * QB, :]).astype(BF16)
    dk_sum[...] = jnp.zeros_like(dk_sum)
    dv_sum[...] = jnp.zeros_like(dv_sum)

    def one_head(h, carry):
        rows = pl.ds(pl.multiple_of(h * HEAD, HEAD), HEAD)
        for i in range(SEQ_LEN // QB):
            lo, hi = max(0, i - 2) * QB, (i + 1) * QB
            here = slice(i * QB, hi)
            q_block = q_all[h, here, :]
            keys = doc_c[lo:hi, :]
            same = jnp.concatenate([keys, keys], axis=1) == doc_row[:, here]
            earlier = lax.broadcasted_iota(jnp.int32, (hi - lo, QB), 0) + lo <= lax.broadcasted_iota(
                jnp.int32, (hi - lo, QB), 1
            ) + i * QB
            scores = jnp.where(same & earlier, nt(k_ref[lo:hi, :], q_block) * SOFT_SCALE, NEG_FILL)
            terms = jnp.exp(scores - jnp.max(scores, axis=0, keepdims=True))
            weights = terms * (1.0 / jnp.sum(terms, axis=0, keepdims=True))
            weights_low = weights.astype(BF16)
            out = nn(v_t[:, lo:hi], weights_low).astype(BF16)
            o_t[rows, here] = out
            grad = g_t[rows, here]
            delta = jnp.sum(grad.astype(F32) * out.astype(F32), axis=0, keepdims=True)
            dscores = (weights * (nn(v_ref[lo:hi, :], grad) - delta)).astype(BF16)
            dq_all[h, here, :] = (nn(k_t[:, lo:hi], dscores) * SOFT_SCALE).T.astype(BF16)
            dk_sum[lo:hi, :] += nn(dscores, q_block)
            dv_sum[lo:hi, :] += nt(weights_low, grad)
        return carry

    lax.fori_loop(0, 2, one_head, 0)
    dk_ref[...] = (dk_sum[...] * SOFT_SCALE).astype(BF16)
    dv_ref[...] = dv_sum[...].astype(BF16)
    for c in range(D // 256):
        cols = slice(c * 256, (c + 1) * 256)
        wo_ref[:, :, :, cols] = nn(o_t[...], g_all[:, cols]).reshape(N_Z, N_X, PACK, 256).astype(BF16)


def backward_exchange(
    dq_all, dk_ref, dv_ref, tag_ref, target_ref, wo_ref,
    dq_out, dk_out, dv_out, wo_out,
    came_q, came_k, came_v, slots_q, slots_kv, ret_q, ret_kv, wo_x, wo_mid, wo_z,
    own, head_send, head_recv, slot_send, slot_recv, wo_send, wo_recv,
):
    s, d = lax.axis_index("seq"), lax.axis_index("dp")
    z, x = d // N_X, lax.rem(d, N_X)
    barrier = greet(s, d)
    kept = [
        pltpu.make_async_copy(dq_all.at[0, s], came_q.at[0, s], own.at[0]),
        pltpu.make_async_copy(dq_all.at[1, s], came_q.at[1, s], own.at[1]),
        pltpu.make_async_copy(dk_ref.at[s], came_k.at[s], own.at[2]),
        pltpu.make_async_copy(dv_ref.at[s], came_v.at[s], own.at[3]),
        pltpu.make_async_copy(wo_ref.at[:, x], wo_x.at[x], own.at[4]),
    ]
    for copy in kept:
        copy.start()
    for copy in kept:
        copy.wait()
    place = tag_ref[...].astype(F32).reshape(N_DP * PACK, TOK).astype(BF16)
    gather = (lax.broadcasted_iota(jnp.int32, (TOK, N_DP * PACK), 1) == target_ref[...]).astype(F32).astype(BF16)
    wait_greeted(barrier)

    for j, (src, dst) in enumerate(
        ((dq_all.at[0], came_q.at[0]), (dq_all.at[1], came_q.at[1]), (dk_ref, came_k), (dv_ref, came_v))
    ):

        def to_owner(i, carry):
            t = lax.rem(s + i, N_SEQ)
            remote(src.at[t], dst.at[s], head_send.at[j], head_recv.at[j], t, d).start()
            return carry

        lax.fori_loop(1, N_SEQ, to_owner, 0)

    def wo_along_x(i, carry):
        xx = lax.rem(x + i, N_X)
        remote(wo_ref.at[:, xx], wo_x.at[x], wo_send.at[0], wo_recv.at[0], s, z * N_X + xx).start()
        return carry

    lax.fori_loop(1, N_X, wo_along_x, 0)

    for h in range(2):
        wait_bytes(came_q.at[h, 0 : N_SEQ - 1], head_recv.at[h])
        for g in range(N_SEQ):
            slots_q[h, :, :, g * HEAD : (g + 1) * HEAD] = as_slots(nn(place, came_q[h, g]))
        send_slots(slots_q.at[h], ret_q.at[h], slot_send.at[h], slot_recv.at[h], s, d)
    wait_bytes(came_k.at[0 : N_SEQ - 1], head_recv.at[2])
    wait_bytes(came_v.at[0 : N_SEQ - 1], head_recv.at[3])
    for part, ref in enumerate((came_k, came_v)):
        for c in range(4):
            both = (ref[2 * c].astype(F32) + ref[2 * c + 1].astype(F32)).astype(BF16)
            cols = slice(part * 512 + c * HEAD, part * 512 + (c + 1) * HEAD)
            slots_kv[:, :, cols] = as_slots(nn(place, both))
    send_slots(slots_kv, ret_kv, slot_send.at[2], slot_recv.at[2], s, d)
    kept = [
        pltpu.make_async_copy(slots_q.at[0, d], ret_q.at[0, d], own.at[0]),
        pltpu.make_async_copy(slots_q.at[1, d], ret_q.at[1, d], own.at[1]),
        pltpu.make_async_copy(slots_kv.at[d], ret_kv.at[d], own.at[2]),
    ]
    for copy in kept:
        copy.start()

    wait_bytes(wo_x.at[0 : N_X - 1], wo_recv.at[0])
    for c in range(D // 256):
        cols = slice(c * 256, (c + 1) * 256)
        total = wo_x[0, :, :, cols].astype(F32)
        for j in range(1, N_X):
            total += wo_x[j, :, :, cols].astype(F32)
        wo_mid[:, :, cols] = total.astype(BF16)

    def wo_along_z(i, carry):
        zz = lax.rem(z + i, N_Z)
        remote(wo_mid.at[zz], wo_z.at[z], wo_send.at[1], wo_recv.at[1], s, zz * N_X + x).start()
        return carry

    lax.fori_loop(1, N_Z, wo_along_z, 0)
    keep = pltpu.make_async_copy(wo_mid.at[z], wo_z.at[z], own.at[3])
    keep.start()
    for copy in kept:
        copy.wait()
    keep.wait()

    for h in range(2):
        wait_bytes(ret_q.at[h, 0 : N_DP - 1], slot_recv.at[h])
        for c in range(4):
            two = nn(gather, slot_rows(ret_q.at[h], slice(c * 256, (c + 1) * 256))).astype(BF16)
            for e in range(2):
                at = (2 * c + e) * 256 + h * HEAD
                dq_out[:, at : at + HEAD] = two[:, e * HEAD : (e + 1) * HEAD]
    wait_bytes(ret_kv.at[0 : N_DP - 1], slot_recv.at[2])
    for part, ref in enumerate((dk_out, dv_out)):
        for c in range(2):
            at = part * 512 + c * 256
            ref[:, c * 256 : (c + 1) * 256] = nn(gather, slot_rows(ret_kv, slice(at, at + 256))).astype(BF16)
    wait_bytes(wo_z.at[0 : N_Z - 1], wo_recv.at[1])
    total = wo_z[0].astype(F32)
    for j in range(1, N_Z):
        total += wo_z[j].astype(F32)
    wo_out[...] = total * GRAD_SCALE

    for h in range(2):
        wait_bytes(ret_q.at[h, 0 : N_DP - 1], slot_send.at[h])
    wait_bytes(ret_kv.at[0 : N_DP - 1], slot_send.at[2])
    for h in range(2):
        wait_bytes(came_q.at[h, 0 : N_SEQ - 1], head_send.at[h])
    wait_bytes(came_k.at[0 : N_SEQ - 1], head_send.at[2])
    wait_bytes(came_v.at[0 : N_SEQ - 1], head_send.at[3])
    wait_bytes(wo_x.at[0 : N_X - 1], wo_send.at[0])
    wait_bytes(wo_z.at[0 : N_Z - 1], wo_send.at[1])


def sds(shape, dtype=BF16):
    return jax.ShapeDtypeStruct(shape, dtype)


def dma(n):
    return pltpu.SemaphoreType.DMA((n,))


def body(q_rows, key_rows, value_rows, pack_peer, pack_slot, doc_ids, grad_out, out_weight):
    in_block = lax.broadcasted_iota(jnp.int32, (16, PACK), 1)
    target = pack_peer[:, None] * PACK + in_block
    landing = pack_slot[:, None] * PACK + in_block
    slot = (N_DP, PACK)
    q_all, k_all, v_all, tag, g_all, w_all = pl.pallas_call(
        forward_exchange,
        name="forward_exchange",
        out_shape=(
            sds((2, N_SEQ, TOK, HEAD)), sds((N_SEQ, TOK, HEAD)), sds((N_SEQ, TOK, HEAD)), sds((*slot, TOK)),
            sds((N_SEQ, TOK, D)), sds((N_Z, N_X, PACK, D)),
        ),
        in_specs=[VMEM] * 7,
        out_specs=(VMEM,) * 6,
        scratch_shapes=[
            pltpu.VMEM((*slot, TOK), BF16), pltpu.VMEM((*slot, KV_COLS), BF16), pltpu.VMEM((2, *slot, KV_COLS), BF16),
            pltpu.VMEM((*slot, KV_COLS), BF16), pltpu.VMEM((2, *slot, KV_COLS), BF16),
            pltpu.VMEM((8, TOK, HEAD), BF16), pltpu.VMEM((2, 8, TOK, HEAD), BF16),
            dma(4), dma(4), dma(4), dma(4), dma(4), dma(8), dma(8), dma(2), dma(2),
        ],
        compiler_params=pltpu.CompilerParams(collective_id=0, has_side_effects=True, vmem_limit_bytes=40 << 20),
    )(q_rows, key_rows, value_rows, target.reshape(1, TOK), landing.reshape(TOK, 1), grad_out[0], out_weight)

    dq_all, dk_part, dv_part, wo_part = pl.pallas_call(
        attention,
        name="attention",
        out_shape=(
            sds((2, SEQ_LEN, HEAD)), sds((SEQ_LEN, HEAD)), sds((SEQ_LEN, HEAD)), sds((N_Z, N_X, PACK, D)),
        ),
        in_specs=[VMEM] * 6,
        out_specs=(VMEM,) * 4,
        scratch_shapes=[
            pltpu.VMEM((2 * HEAD, SEQ_LEN), BF16), pltpu.VMEM((2 * HEAD, SEQ_LEN), BF16),
            pltpu.VMEM((HEAD, SEQ_LEN), BF16), pltpu.VMEM((HEAD, SEQ_LEN), BF16),
            pltpu.VMEM((SEQ_LEN, HEAD), F32), pltpu.VMEM((SEQ_LEN, HEAD), F32), pltpu.VMEM((SEQ_LEN, HEAD), F32),
        ],
        compiler_params=pltpu.CompilerParams(vmem_limit_bytes=40 << 20),
    )(
        q_all.reshape(2, SEQ_LEN, HEAD), k_all.reshape(SEQ_LEN, HEAD), v_all.reshape(SEQ_LEN, HEAD),
        g_all.reshape(SEQ_LEN, D), w_all, doc_ids,
    )

    return pl.pallas_call(
        backward_exchange,
        name="backward_exchange",
        out_shape=(sds((TOK, D)), sds((TOK, 512)), sds((TOK, 512)), sds((PACK, D), F32)),
        in_specs=[VMEM] * 6,
        out_specs=(VMEM,) * 4,
        scratch_shapes=[
            pltpu.VMEM((2, N_SEQ, TOK, HEAD), BF16), pltpu.VMEM((N_SEQ, TOK, HEAD), BF16),
            pltpu.VMEM((N_SEQ, TOK, HEAD), BF16), pltpu.VMEM((2, *slot, KV_COLS), BF16),
            pltpu.VMEM((*slot, KV_COLS), BF16), pltpu.VMEM((2, *slot, KV_COLS), BF16), pltpu.VMEM((*slot, KV_COLS), BF16),
            pltpu.VMEM((N_X, N_Z, PACK, D), BF16), pltpu.VMEM((N_Z, PACK, D), BF16), pltpu.VMEM((N_Z, PACK, D), BF16),
            dma(5), dma(4), dma(4), dma(3), dma(3), dma(2), dma(2),
        ],
        compiler_params=pltpu.CompilerParams(collective_id=1, has_side_effects=True, vmem_limit_bytes=40 << 20),
    )(
        dq_all.reshape(2, N_SEQ, TOK, HEAD), dk_part.reshape(N_SEQ, TOK, HEAD), dv_part.reshape(N_SEQ, TOK, HEAD),
        tag, target.reshape(TOK, 1), wo_part,
    )


def solution(mesh):
    return jax.shard_map(
        body,
        mesh=mesh,
        in_specs=(
            P(("seq", "dp"), None),
            P(("seq", "dp"), None),
            P(("seq", "dp"), None),
            P(("seq", "dp")),
            P(("seq", "dp")),
            P("dp", None),
            P("dp", "seq", None),
            P(("seq", "dp"), None),
        ),
        out_specs=(
            P(("seq", "dp"), None),
            P(("seq", "dp"), None),
            P(("seq", "dp"), None),
            P(("seq", "dp"), None),
        ),
        check_vma=False,
    )
```

```python
import math

import jax
import jax.numpy as jnp
from jax import lax
from jax.experimental import pallas as pl
from jax.experimental.pallas import tpu as pltpu
from jax.sharding import PartitionSpec as P

HEAD = 128
PACK = 8
NEG_FILL = -1e30
MESH = pl.DeviceIdType.MESH
BF16 = jnp.bfloat16
F32 = jnp.float32
N_SEQ, N_Y = 8, 4
N_DP, N_Z, N_X = 32, 8, 4
TOK = 128
SEQ_LEN = 1024
D = 2048
KV_COLS = 1024
QB = 256
SOFT_SCALE = 1.0 / math.sqrt(HEAD)
GRAD_SCALE = 8.0 / math.sqrt(N_DP * SEQ_LEN)
VMEM = pl.BlockSpec(memory_space=pltpu.VMEM)
ANY = pl.BlockSpec(memory_space=pl.ANY)


def nn(a, b):
    return lax.dot_general(a, b, (((1,), (0,)), ((), ())), preferred_element_type=F32)


def nt(a, b):
    return lax.dot_general(a, b, (((1,), (1,)), ((), ())), preferred_element_type=F32)


def remote(src, dst, send, recv, seq, dp):
    return pltpu.make_async_remote_copy(
        src_ref=src, dst_ref=dst, send_sem=send, recv_sem=recv, device_id=(seq, dp), device_id_type=MESH
    )


def greet(s, d):
    barrier = pltpu.get_barrier_semaphore()

    def along_dp(i, carry):
        pl.semaphore_signal(barrier, inc=1, device_id=(s, lax.rem(d + i, N_DP)), device_id_type=MESH)
        return carry

    def along_seq(i, carry):
        pl.semaphore_signal(barrier, inc=1, device_id=(lax.rem(s + i, N_SEQ), d), device_id_type=MESH)
        return carry

    lax.fori_loop(1, N_DP, along_dp, 0)
    lax.fori_loop(1, N_SEQ, along_seq, 0)
    return barrier


def wait_greeted(barrier):
    pl.semaphore_wait(barrier, N_DP - 1 + N_SEQ - 1)


def send_slots(slots, came, send, recv, s, d):
    def one(i, carry):
        p = lax.rem(d + i, N_DP)
        remote(slots.at[p], came.at[d], send, recv, s, p).start()
        return carry

    lax.fori_loop(1, N_DP, one, 0)


def wait_bytes(ref, sem):
    pltpu.make_async_copy(ref, ref, sem).wait()


def slot_rows(ref, columns):
    block = ref[:, :, columns]
    return block.astype(F32).reshape(N_DP * PACK, block.shape[2]).astype(BF16)


def as_slots(rows):
    return rows.reshape(N_DP, PACK, rows.shape[1]).astype(BF16)


def each_other(count, me, send):
    def one(i, carry):
        send(lax.rem(me + i, count))
        return carry

    lax.fori_loop(1, count, one, 0)


def rows_of(values, scalars, width):
    chosen = jnp.zeros_like(values)
    for i in range(TOK // PACK):
        chosen = jnp.where(values == i, scalars[i], chosen)
    return chosen * PACK + width


def kernel(
    q_hbm, k_hbm, v_hbm, peer_hbm, slot_hbm, doc_hbm, grad_hbm, w_hbm,
    dq_out, dk_out, dv_out, wo_out,
    peer, slot, q_in, k_in, v_in, doc_in, g_all, w_all,
    slots_kv, slots_q, came_kv, came_q, packed_kv, packed_q, q_all, k_all, v_all,
    g_t, o_t, k_t, v_t, doc_c, dk_sum, dv_sum, dq_all, dk_part, dv_part,
    back_q, back_k, back_v, out_q, out_kv, ret_q, ret_kv, wo_part, wo_x, wo_mid, wo_z,
    own, slot_send, slot_recv, head_send, head_recv, g_send, g_recv, w_send, w_recv,
    back_send, back_recv, out_send, ret_recv, wo_send, wo_recv,
):
    s, d = lax.axis_index("seq"), lax.axis_index("dp")
    y, core = s // 2, lax.rem(s, 2)
    z, x = d // N_X, lax.rem(d, N_X)
    mate = y * 2 + 1 - core
    up, down = lax.rem(y + 1, N_Y) * 2 + core, lax.rem(y + N_Y - 1, N_Y) * 2 + core
    across = lax.rem(y + 2, N_Y) * 2 + core

    inputs = [
        pltpu.make_async_copy(src, dst, own.at[i])
        for i, (src, dst) in enumerate(
            (
                (peer_hbm, peer), (slot_hbm, slot), (k_hbm, k_in), (v_hbm, v_in), (w_hbm, w_all.at[z, x]),
                (grad_hbm.at[0], g_all.at[s]), (q_hbm, q_in), (doc_hbm, doc_in),
            )
        )
    ]
    for copy in inputs:
        copy.start()
    barrier = greet(s, d)

    inputs[0].wait()
    inputs[1].wait()
    lane = lax.broadcasted_iota(jnp.int32, (1, TOK), 1)
    target = rows_of(lane // PACK, peer, lax.rem(lane, PACK))
    place = (lax.broadcasted_iota(jnp.int32, (N_DP * PACK, TOK), 0) == target).astype(F32).astype(BF16)
    row = lax.broadcasted_iota(jnp.int32, (TOK, TOK), 0)
    landing = rows_of(row // PACK, slot, lax.rem(row, PACK))
    tags = (lax.broadcasted_iota(jnp.int32, (TOK, TOK), 1) == landing).astype(F32).astype(BF16)
    slots_kv[:, :, KV_COLS:] = as_slots(nn(place, tags))
    inputs[2].wait()
    inputs[3].wait()
    for part, ref in enumerate((k_in, v_in)):
        for c in range(2):
            cols = slice(part * 512 + c * 256, part * 512 + (c + 1) * 256)
            slots_kv[:, :, cols] = as_slots(nn(place, ref[:, c * 256 : (c + 1) * 256]))
    inputs[4].wait()
    inputs[5].wait()
    wait_greeted(barrier)

    each_other(N_Z, z, lambda p: remote(w_all.at[z, x], w_all.at[z, x], w_send.at[0], w_recv.at[0], s, p * N_X + x).start())
    g_up = remote(g_all.at[s], g_all.at[s], g_send.at[0], g_recv.at[0], up, d)
    g_down = remote(g_all.at[s], g_all.at[s], g_send.at[1], g_recv.at[1], down, d)
    g_mate = remote(g_all.at[s], g_all.at[s], g_send.at[2], g_recv.at[2], mate, d)
    g_up.start()
    g_down.start()
    g_mate.start()
    send_slots(slots_kv, came_kv, slot_send.at[0], slot_recv.at[0], s, d)

    inputs[6].wait()
    inputs[7].wait()
    for g in range(N_SEQ):
        both = nn(place, q_in[:, g * 256 : (g + 1) * 256])
        slots_q[0, :, :, g * HEAD : (g + 1) * HEAD] = as_slots(both[:, :HEAD])
        slots_q[1, :, :, g * HEAD : (g + 1) * HEAD] = as_slots(both[:, HEAD:])
    for h in range(2):
        send_slots(slots_q.at[h], came_q.at[h], slot_send.at[1 + h], slot_recv.at[1 + h], s, d)
    kept = [
        pltpu.make_async_copy(slots_kv.at[d], came_kv.at[d], own.at[0]),
        pltpu.make_async_copy(slots_q.at[0, d], came_q.at[0, d], own.at[1]),
        pltpu.make_async_copy(slots_q.at[1, d], came_q.at[1, d], own.at[2]),
    ]
    for copy in kept:
        copy.start()

    doc_row = doc_in[...].astype(F32)
    doc_c[...] = jnp.broadcast_to(doc_row, (HEAD, SEQ_LEN)).T
    dk_sum[...] = jnp.zeros_like(dk_sum)
    dv_sum[...] = jnp.zeros_like(dv_sum)
    for copy in kept:
        copy.wait()

    wait_bytes(w_all.at[0 : N_Z - 1, 0], w_recv.at[0])
    wait_bytes(w_all.at[0 : N_Z - 1, 0], w_send.at[0])
    each_other(N_X, x, lambda p: remote(w_all.at[:, x], w_all.at[:, x], w_send.at[1], w_recv.at[1], s, z * N_X + p).start())

    g_up.wait_recv()
    from_down = g_all.at[down]
    half_up = remote(from_down.at[0:64], from_down.at[0:64], g_send.at[3], g_recv.at[3], up, d)
    mate_down = remote(from_down, from_down, g_send.at[4], g_recv.at[4], mate, d)
    half_up.start()
    mate_down.start()
    g_down.wait_recv()
    from_up = g_all.at[up]
    half_down = remote(from_up.at[64:128], from_up.at[64:128], g_send.at[5], g_recv.at[5], down, d)
    mate_up = remote(from_up, from_up, g_send.at[6], g_recv.at[6], mate, d)
    half_down.start()
    mate_up.start()

    wait_bytes(came_kv.at[0 : N_DP - 1], slot_recv.at[0])
    tag_rows = came_kv[:, :, KV_COLS:].astype(F32).reshape(N_DP * PACK, TOK)
    scatter = tag_rows.astype(BF16)
    gather = tag_rows.T.astype(BF16)
    for c in range(4):
        two = nn(gather, slot_rows(came_kv, slice(c * 256, (c + 1) * 256))).astype(BF16)
        packed_kv[2 * c] = two[:, :HEAD]
        packed_kv[2 * c + 1] = two[:, HEAD:]

    def keys_out(t):
        remote(packed_kv.at[t // 2], k_all.at[s], head_send.at[0], head_recv.at[0], t, d).start()
        remote(packed_kv.at[4 + t // 2], v_all.at[s], head_send.at[1], head_recv.at[1], t, d).start()

    each_other(N_SEQ, s, keys_out)
    kept = [
        pltpu.make_async_copy(packed_kv.at[s // 2], k_all.at[s], own.at[0]),
        pltpu.make_async_copy(packed_kv.at[4 + s // 2], v_all.at[s], own.at[1]),
    ]
    for copy in kept:
        copy.start()

    half_up.wait_recv()
    half_down.wait_recv()
    from_across = g_all.at[across]
    mate_across = remote(from_across, from_across, g_send.at[7], g_recv.at[7], mate, d)
    mate_across.start()

    for copy in kept:
        copy.wait()
    wait_bytes(k_all.at[0 : N_SEQ - 1], head_recv.at[0])
    wait_bytes(v_all.at[0 : N_SEQ - 1], head_recv.at[1])
    k_t[...] = k_all[...].reshape(SEQ_LEN, HEAD).astype(F32).T.astype(BF16)
    v_t[...] = v_all[...].reshape(SEQ_LEN, HEAD).astype(F32).T.astype(BF16)
    for copy in (g_mate, mate_down, mate_up, mate_across):
        copy.wait_recv()
    wait_bytes(w_all.at[:, 0 : N_X - 1], w_recv.at[1])
    weight = w_all[...].astype(F32).reshape(2 * HEAD, D).astype(BF16)
    for i in range(SEQ_LEN // QB):
        g_t[:, i * QB : (i + 1) * QB] = nt(weight, g_all[2 * i : 2 * i + 2].reshape(QB, D)).astype(BF16)

    def queries_in(h):
        wait_bytes(came_q.at[h, 0 : N_DP - 1], slot_recv.at[1 + h])
        for c in range(4):
            two = nn(gather, slot_rows(came_q.at[h], slice(c * 256, (c + 1) * 256))).astype(BF16)
            packed_q[h, 2 * c] = two[:, :HEAD]
            packed_q[h, 2 * c + 1] = two[:, HEAD:]
        each_other(
            N_SEQ, s, lambda t: remote(packed_q.at[h, t], q_all.at[h, s], head_send.at[2 + h], head_recv.at[2 + h], t, d).start()
        )
        keep = pltpu.make_async_copy(packed_q.at[h, s], q_all.at[h, s], own.at[2 + h])
        keep.start()
        return keep

    def one_head(h):
        rows = slice(h * HEAD, (h + 1) * HEAD)
        for i in range(SEQ_LEN // QB):
            first, last = 2 * max(0, i - 2), 2 * (i + 1)
            lo, hi = first * TOK, last * TOK
            here = slice(i * QB, hi)
            q_block = q_all[h, 2 * i : 2 * i + 2].reshape(QB, HEAD)
            k_block = k_all[first:last].reshape(hi - lo, HEAD)
            v_block = v_all[first:last].reshape(hi - lo, HEAD)
            keys = doc_c[lo:hi, :]
            same = jnp.concatenate([keys, keys], axis=1) == doc_row[:, here]
            earlier = lax.broadcasted_iota(jnp.int32, (hi - lo, QB), 0) + lo <= lax.broadcasted_iota(
                jnp.int32, (hi - lo, QB), 1
            ) + i * QB
            scores = jnp.where(same & earlier, nt(k_block, q_block) * SOFT_SCALE, NEG_FILL)
            terms = jnp.exp(scores - jnp.max(scores, axis=0, keepdims=True))
            weights = terms * (1.0 / jnp.sum(terms, axis=0, keepdims=True))
            weights_low = weights.astype(BF16)
            out = nn(v_t[:, lo:hi], weights_low).astype(BF16)
            o_t[rows, here] = out
            grad = g_t[rows, here]
            delta = jnp.sum(grad.astype(F32) * out.astype(F32), axis=0, keepdims=True)
            dscores = (weights * (nn(v_block, grad) - delta)).astype(BF16)
            dq_block = (nn(k_t[:, lo:hi], dscores) * SOFT_SCALE).T.astype(BF16)
            dq_all[h, 2 * i] = dq_block[:TOK]
            dq_all[h, 2 * i + 1] = dq_block[TOK:]
            dk_sum[lo:hi, :] += nn(dscores, q_block)
            dv_sum[lo:hi, :] += nt(weights_low, grad)

    def to_owners(src, dst, j):
        each_other(N_SEQ, s, lambda t: remote(src.at[t], dst.at[s], back_send.at[j], back_recv.at[j], t, d).start())
        keep = pltpu.make_async_copy(src.at[s], dst.at[s], own.at[4 + j])
        keep.start()
        return keep

    def arrived(keep, dst, j):
        keep.wait()
        wait_bytes(dst.at[0 : N_SEQ - 1], back_recv.at[j])

    def wo_half(h):
        part = slice(4 * h, 4 * h + 4)
        for c in range(D // 256):
            cols = slice(c * 256, (c + 1) * 256)
            product = nn(o_t[h * HEAD : (h + 1) * HEAD, :], g_all[:, :, cols].reshape(SEQ_LEN, 256))
            wo_part[part, :, :, cols] = product.reshape(4, N_X, PACK, 256).astype(BF16)
        each_other(
            N_X, x, lambda p: remote(wo_part.at[part, p], wo_x.at[x, part], wo_send.at[h], wo_recv.at[h], s, z * N_X + p).start()
        )
        keep = pltpu.make_async_copy(wo_part.at[part, x], wo_x.at[x, part], own.at[h])
        keep.start()
        return keep

    def wo_half_sum(h, keep):
        part = slice(4 * h, 4 * h + 4)
        keep.wait()
        wait_bytes(wo_x.at[0 : N_X - 1, part], wo_recv.at[h])
        for c in range(D // 256):
            cols = slice(c * 256, (c + 1) * 256)
            total = wo_x[0, part, :, cols].astype(F32)
            for j in range(1, N_X):
                total += wo_x[j, part, :, cols].astype(F32)
            wo_mid[part, :, cols] = total.astype(BF16)
        for zz in range(4 * h, 4 * h + 4):

            @pl.when(z != zz)
            def _():
                remote(wo_mid.at[zz], wo_z.at[z], wo_send.at[2], wo_recv.at[2], s, zz * N_X + x).start()

    def queries_back(h, keep):
        arrived(keep, back_q.at[h], h)
        for g in range(N_SEQ):
            out_q[h, :, :, g * HEAD : (g + 1) * HEAD] = as_slots(nn(scatter, back_q[h, g]))
        send_slots(out_q.at[h], ret_q.at[h], out_send.at[h], ret_recv.at[h], s, d)
        keep = pltpu.make_async_copy(out_q.at[h, d], ret_q.at[h, d], own.at[2 + h])
        keep.start()
        return keep

    keep_q0 = queries_in(0)
    keep_q0.wait()
    wait_bytes(q_all.at[0, 0 : N_SEQ - 1], head_recv.at[2])
    one_head(0)
    keep_back0 = to_owners(dq_all.at[0], back_q.at[0], 0)
    keep_q1 = queries_in(1)
    keep_ret0 = queries_back(0, keep_back0)
    keep_wo0 = wo_half(0)
    keep_q1.wait()
    wait_bytes(q_all.at[1, 0 : N_SEQ - 1], head_recv.at[3])
    one_head(1)
    keep_back1 = to_owners(dq_all.at[1], back_q.at[1], 1)
    dk_part[...] = (dk_sum[...] * SOFT_SCALE).astype(BF16).reshape(N_SEQ, TOK, HEAD)
    keep_k = to_owners(dk_part, back_k, 2)
    dv_part[...] = dv_sum[...].astype(BF16).reshape(N_SEQ, TOK, HEAD)
    keep_v = to_owners(dv_part, back_v, 3)
    wo_half_sum(0, keep_wo0)
    keep_wo1 = wo_half(1)
    keep_ret1 = queries_back(1, keep_back1)
    arrived(keep_k, back_k, 2)
    arrived(keep_v, back_v, 3)
    for part, ref in enumerate((back_k, back_v)):
        for c in range(4):
            both = (ref[2 * c].astype(F32) + ref[2 * c + 1].astype(F32)).astype(BF16)
            cols = slice(part * 512 + c * HEAD, part * 512 + (c + 1) * HEAD)
            out_kv[:, :, cols] = as_slots(nn(scatter, both))
    send_slots(out_kv, ret_kv, out_send.at[2], ret_recv.at[2], s, d)
    keep_kv = pltpu.make_async_copy(out_kv.at[d], ret_kv.at[d], own.at[4])
    keep_kv.start()
    wo_half_sum(1, keep_wo1)
    keep_mid = pltpu.make_async_copy(wo_mid.at[z], wo_z.at[z], own.at[5])
    keep_mid.start()

    column = lax.broadcasted_iota(jnp.int32, (TOK, N_DP * PACK), 0)
    target = rows_of(column // PACK, peer, lax.rem(column, PACK))
    pick = (lax.broadcasted_iota(jnp.int32, (TOK, N_DP * PACK), 1) == target).astype(F32).astype(BF16)
    for h, keep in enumerate((keep_ret0, keep_ret1)):
        keep.wait()
        wait_bytes(ret_q.at[h, 0 : N_DP - 1], ret_recv.at[h])
        for c in range(4):
            two = nn(pick, slot_rows(ret_q.at[h], slice(c * 256, (c + 1) * 256))).astype(BF16)
            for e in range(2):
                at = (2 * c + e) * 256 + h * HEAD
                dq_out[:, at : at + HEAD] = two[:, e * HEAD : (e + 1) * HEAD]
    keep_kv.wait()
    wait_bytes(ret_kv.at[0 : N_DP - 1], ret_recv.at[2])
    for part, ref in enumerate((dk_out, dv_out)):
        for c in range(2):
            at = part * 512 + c * 256
            ref[:, c * 256 : (c + 1) * 256] = nn(pick, slot_rows(ret_kv, slice(at, at + 256))).astype(BF16)
    keep_mid.wait()
    wait_bytes(wo_z.at[0 : N_Z - 1], wo_recv.at[2])
    total = wo_z[0].astype(F32)
    for j in range(1, N_Z):
        total += wo_z[j].astype(F32)
    wo_out[...] = total * GRAD_SCALE

    for copy in (g_up, g_down, g_mate, half_up, mate_down, half_down, mate_up, mate_across):
        copy.wait_send()
    wait_bytes(w_all.at[:, 0 : N_X - 1], w_send.at[1])
    wait_bytes(came_kv.at[0 : N_DP - 1], slot_send.at[0])
    wait_bytes(k_all.at[0 : N_SEQ - 1], head_send.at[0])
    wait_bytes(v_all.at[0 : N_SEQ - 1], head_send.at[1])
    wait_bytes(back_k.at[0 : N_SEQ - 1], back_send.at[2])
    wait_bytes(back_v.at[0 : N_SEQ - 1], back_send.at[3])
    wait_bytes(ret_kv.at[0 : N_DP - 1], out_send.at[2])
    wait_bytes(wo_z.at[0 : N_Z - 1], wo_send.at[2])
    for h in range(2):
        wait_bytes(came_q.at[h, 0 : N_DP - 1], slot_send.at[1 + h])
        wait_bytes(q_all.at[h, 0 : N_SEQ - 1], head_send.at[2 + h])
        wait_bytes(back_q.at[h, 0 : N_SEQ - 1], back_send.at[h])
        wait_bytes(ret_q.at[h, 0 : N_DP - 1], out_send.at[h])
        wait_bytes(wo_x.at[0 : N_X - 1, 4 * h : 4 * h + 4], wo_send.at[h])


def body(q_rows, key_rows, value_rows, pack_peer, pack_slot, doc_ids, grad_out, out_weight):
    def sds(shape, dtype=BF16):
        return jax.ShapeDtypeStruct(shape, dtype)

    def buf(*shape, dtype=BF16):
        return pltpu.VMEM(shape, dtype)

    slot = (N_DP, PACK)
    heads = (N_SEQ, TOK, HEAD)
    return pl.pallas_call(
        kernel,
        name="attention_backward",
        out_shape=(sds((TOK, D)), sds((TOK, 512)), sds((TOK, 512)), sds((PACK, D), F32)),
        in_specs=[ANY] * 8,
        out_specs=(VMEM,) * 4,
        scratch_shapes=[
            pltpu.SMEM((16,), jnp.int32), pltpu.SMEM((16,), jnp.int32),
            buf(TOK, D), buf(TOK, 512), buf(TOK, 512), buf(1, SEQ_LEN, dtype=jnp.int32),
            buf(N_SEQ, TOK, D), buf(N_Z, N_X, PACK, D),
            buf(*slot, KV_COLS + TOK), buf(2, *slot, KV_COLS), buf(*slot, KV_COLS + TOK), buf(2, *slot, KV_COLS),
            buf(*heads), buf(2, *heads), buf(2, *heads), buf(*heads), buf(*heads),
            buf(2 * HEAD, SEQ_LEN), buf(2 * HEAD, SEQ_LEN), buf(HEAD, SEQ_LEN), buf(HEAD, SEQ_LEN),
            buf(SEQ_LEN, HEAD, dtype=F32), buf(SEQ_LEN, HEAD, dtype=F32), buf(SEQ_LEN, HEAD, dtype=F32),
            buf(2, *heads), buf(*heads), buf(*heads),
            buf(2, *heads), buf(*heads), buf(*heads),
            buf(2, *slot, KV_COLS), buf(*slot, KV_COLS), buf(2, *slot, KV_COLS), buf(*slot, KV_COLS),
            buf(N_Z, N_X, PACK, D), buf(N_X, N_Z, PACK, D), buf(N_Z, PACK, D), buf(N_Z, PACK, D),
            *(pltpu.SemaphoreType.DMA((n,)) for n in (8, 3, 3, 4, 4, 8, 8, 2, 2, 4, 4, 3, 3, 3, 3)),
        ],
        compiler_params=pltpu.CompilerParams(collective_id=0, has_side_effects=True, vmem_limit_bytes=60 << 20),
    )(q_rows, key_rows, value_rows, pack_peer, pack_slot, doc_ids, grad_out, out_weight)


def solution(mesh):
    return jax.shard_map(
        body,
        mesh=mesh,
        in_specs=(
            P(("seq", "dp"), None),
            P(("seq", "dp"), None),
            P(("seq", "dp"), None),
            P(("seq", "dp")),
            P(("seq", "dp")),
            P("dp", None),
            P("dp", "seq", None),
            P(("seq", "dp"), None),
        ),
        out_specs=(
            P(("seq", "dp"), None),
            P(("seq", "dp"), None),
            P(("seq", "dp"), None),
            P(("seq", "dp"), None),
        ),
        check_vma=False,
    )
```

```python
import math

import jax
import jax.numpy as jnp
from jax import lax
from jax.experimental import pallas as pl
from jax.experimental.pallas import tpu as pltpu
from jax.sharding import PartitionSpec as P

HEAD = 128
PACK = 8
NEG_FILL = -1e30
MESH = pl.DeviceIdType.MESH
BF16 = jnp.bfloat16
F32 = jnp.float32
N_SEQ, N_Y = 8, 4
N_DP, N_Z, N_X = 32, 8, 4
TOK = 128
SEQ_LEN = 1024
D = 2048
KV_COLS = 1024
QB = 256
SOFT_SCALE = 1.0 / math.sqrt(HEAD)
GRAD_SCALE = 8.0 / math.sqrt(N_DP * SEQ_LEN)
VMEM = pl.BlockSpec(memory_space=pltpu.VMEM)
ANY = pl.BlockSpec(memory_space=pl.ANY)


def nn(a, b):
    return lax.dot_general(a, b, (((1,), (0,)), ((), ())), preferred_element_type=F32)


def nt(a, b):
    return lax.dot_general(a, b, (((1,), (1,)), ((), ())), preferred_element_type=F32)


def remote(src, dst, send, recv, seq, dp):
    return pltpu.make_async_remote_copy(
        src_ref=src, dst_ref=dst, send_sem=send, recv_sem=recv, device_id=(seq, dp), device_id_type=MESH
    )


def greet(s, d):
    barrier = pltpu.get_barrier_semaphore()

    def along_dp(i, carry):
        pl.semaphore_signal(barrier, inc=1, device_id=(s, lax.rem(d + i, N_DP)), device_id_type=MESH)
        return carry

    def along_seq(i, carry):
        pl.semaphore_signal(barrier, inc=1, device_id=(lax.rem(s + i, N_SEQ), d), device_id_type=MESH)
        return carry

    lax.fori_loop(1, N_DP, along_dp, 0)
    lax.fori_loop(1, N_SEQ, along_seq, 0)
    return barrier


def wait_greeted(barrier):
    pl.semaphore_wait(barrier, N_DP - 1 + N_SEQ - 1)


def send_slots(slots, came, send, recv, s, d):
    def one(i, carry):
        p = lax.rem(d + i, N_DP)
        remote(slots.at[p], came.at[d], send, recv, s, p).start()
        return carry

    lax.fori_loop(1, N_DP, one, 0)


def wait_bytes(ref, sem):
    pltpu.make_async_copy(ref, ref, sem).wait()


def slot_rows(ref, columns):
    block = ref[:, :, columns]
    return block.astype(F32).reshape(N_DP * PACK, block.shape[2]).astype(BF16)


def as_slots(rows):
    return rows.reshape(N_DP, PACK, rows.shape[1]).astype(BF16)


def each_other(count, me, send):
    def one(i, carry):
        send(lax.rem(me + i, count))
        return carry

    lax.fori_loop(1, count, one, 0)


def rows_of(values, scalars, width):
    chosen = jnp.zeros_like(values)
    for i in range(TOK // PACK):
        chosen = jnp.where(values == i, scalars[i], chosen)
    return chosen * PACK + width


def kernel(
    q_hbm, k_hbm, v_hbm, peer_hbm, slot_hbm, doc_hbm, grad_hbm, w_hbm,
    dq_out, dk_out, dv_out, wo_out,
    peer, slot, q_in, k_in, v_in, doc_in, g_all, w_all,
    slots_kv, slots_q, came_kv, came_q, packed_kv, packed_q, q_all, k_all, v_all,
    g_t, o_t, k_t, v_t, doc_c, dk_sum, dv_sum, dq_all, dk_part, dv_part,
    back_q, back_k, back_v, out_q, out_kv, ret_q, ret_kv, wo_part, wo_x, wo_mid, wo_z,
    own, slot_send, slot_recv, head_send, head_recv, g_send, g_recv, w_send, w_recv,
    back_send, back_recv, out_send, ret_recv, wo_send, wo_recv,
):
    s, d = lax.axis_index("seq"), lax.axis_index("dp")
    y, core = s // 2, lax.rem(s, 2)
    z, x = d // N_X, lax.rem(d, N_X)
    mate = y * 2 + 1 - core
    up, down = lax.rem(y + 1, N_Y) * 2 + core, lax.rem(y + N_Y - 1, N_Y) * 2 + core
    across = lax.rem(y + 2, N_Y) * 2 + core

    inputs = [
        pltpu.make_async_copy(src, dst, own.at[i])
        for i, (src, dst) in enumerate(
            (
                (peer_hbm, peer), (slot_hbm, slot), (k_hbm, k_in), (v_hbm, v_in), (w_hbm, w_all.at[z, x]),
                (grad_hbm.at[0], g_all.at[s]), (q_hbm, q_in), (doc_hbm, doc_in),
            )
        )
    ]
    for copy in inputs:
        copy.start()
    barrier = greet(s, d)

    inputs[4].wait()
    inputs[5].wait()
    wait_greeted(barrier)

    each_other(N_Z, z, lambda p: remote(w_all.at[z, x], w_all.at[z, x], w_send.at[0], w_recv.at[0], s, p * N_X + x).start())
    g_up = remote(g_all.at[s], g_all.at[s], g_send.at[0], g_recv.at[0], up, d)
    g_down = remote(g_all.at[s], g_all.at[s], g_send.at[1], g_recv.at[1], down, d)
    g_mate = remote(g_all.at[s], g_all.at[s], g_send.at[2], g_recv.at[2], mate, d)
    g_up.start()
    g_down.start()
    g_mate.start()

    inputs[0].wait()
    inputs[1].wait()
    lane = lax.broadcasted_iota(jnp.int32, (1, TOK), 1)
    target = rows_of(lane // PACK, peer, lax.rem(lane, PACK))
    place = (lax.broadcasted_iota(jnp.int32, (N_DP * PACK, TOK), 0) == target).astype(F32).astype(BF16)
    row = lax.broadcasted_iota(jnp.int32, (TOK, TOK), 0)
    landing = rows_of(row // PACK, slot, lax.rem(row, PACK))
    tags = (lax.broadcasted_iota(jnp.int32, (TOK, TOK), 1) == landing).astype(F32).astype(BF16)
    slots_kv[:, :, KV_COLS:] = as_slots(nn(place, tags))
    inputs[2].wait()
    inputs[3].wait()
    for part, ref in enumerate((k_in, v_in)):
        for c in range(2):
            cols = slice(part * 512 + c * 256, part * 512 + (c + 1) * 256)
            slots_kv[:, :, cols] = as_slots(nn(place, ref[:, c * 256 : (c + 1) * 256]))
    send_slots(slots_kv, came_kv, slot_send.at[0], slot_recv.at[0], s, d)

    inputs[6].wait()
    inputs[7].wait()
    for g in range(N_SEQ):
        both = nn(place, q_in[:, g * 256 : (g + 1) * 256])
        slots_q[0, :, :, g * HEAD : (g + 1) * HEAD] = as_slots(both[:, :HEAD])
        slots_q[1, :, :, g * HEAD : (g + 1) * HEAD] = as_slots(both[:, HEAD:])
    for h in range(2):
        send_slots(slots_q.at[h], came_q.at[h], slot_send.at[1 + h], slot_recv.at[1 + h], s, d)
    kept = [
        pltpu.make_async_copy(slots_kv.at[d], came_kv.at[d], own.at[0]),
        pltpu.make_async_copy(slots_q.at[0, d], came_q.at[0, d], own.at[1]),
        pltpu.make_async_copy(slots_q.at[1, d], came_q.at[1, d], own.at[2]),
    ]
    for copy in kept:
        copy.start()

    doc_row = doc_in[...].astype(F32)
    doc_c[...] = jnp.broadcast_to(doc_row, (HEAD, SEQ_LEN)).T
    dk_sum[...] = jnp.zeros_like(dk_sum)
    dv_sum[...] = jnp.zeros_like(dv_sum)
    for copy in kept:
        copy.wait()

    wait_bytes(w_all.at[0 : N_Z - 1, 0], w_recv.at[0])
    wait_bytes(w_all.at[0 : N_Z - 1, 0], w_send.at[0])
    each_other(N_X, x, lambda p: remote(w_all.at[:, x], w_all.at[:, x], w_send.at[1], w_recv.at[1], s, z * N_X + p).start())

    g_up.wait_recv()
    from_down = g_all.at[down]
    half_up = remote(from_down.at[0:64], from_down.at[0:64], g_send.at[3], g_recv.at[3], up, d)
    mate_down = remote(from_down, from_down, g_send.at[4], g_recv.at[4], mate, d)
    half_up.start()
    mate_down.start()
    g_down.wait_recv()
    from_up = g_all.at[up]
    half_down = remote(from_up.at[64:128], from_up.at[64:128], g_send.at[5], g_recv.at[5], down, d)
    mate_up = remote(from_up, from_up, g_send.at[6], g_recv.at[6], mate, d)
    half_down.start()
    mate_up.start()

    wait_bytes(came_kv.at[0 : N_DP - 1], slot_recv.at[0])
    tag_rows = came_kv[:, :, KV_COLS:].astype(F32).reshape(N_DP * PACK, TOK)
    scatter = tag_rows.astype(BF16)
    gather = tag_rows.T.astype(BF16)
    for c in range(4):
        two = nn(gather, slot_rows(came_kv, slice(c * 256, (c + 1) * 256))).astype(BF16)
        packed_kv[2 * c] = two[:, :HEAD]
        packed_kv[2 * c + 1] = two[:, HEAD:]

    def keys_out(t):
        remote(packed_kv.at[t // 2], k_all.at[s], head_send.at[0], head_recv.at[0], t, d).start()
        remote(packed_kv.at[4 + t // 2], v_all.at[s], head_send.at[1], head_recv.at[1], t, d).start()

    each_other(N_SEQ, s, keys_out)
    kept = [
        pltpu.make_async_copy(packed_kv.at[s // 2], k_all.at[s], own.at[0]),
        pltpu.make_async_copy(packed_kv.at[4 + s // 2], v_all.at[s], own.at[1]),
    ]
    for copy in kept:
        copy.start()

    half_up.wait_recv()
    half_down.wait_recv()
    from_across = g_all.at[across]
    mate_across = remote(from_across, from_across, g_send.at[7], g_recv.at[7], mate, d)
    mate_across.start()

    for copy in kept:
        copy.wait()
    wait_bytes(k_all.at[0 : N_SEQ - 1], head_recv.at[0])
    wait_bytes(v_all.at[0 : N_SEQ - 1], head_recv.at[1])
    k_t[...] = k_all[...].reshape(SEQ_LEN, HEAD).astype(F32).T.astype(BF16)
    v_t[...] = v_all[...].reshape(SEQ_LEN, HEAD).astype(F32).T.astype(BF16)
    for copy in (g_mate, mate_down, mate_up, mate_across):
        copy.wait_recv()
    wait_bytes(w_all.at[:, 0 : N_X - 1], w_recv.at[1])
    weight = w_all[...].astype(F32).reshape(2 * HEAD, D).astype(BF16)
    for i in range(SEQ_LEN // QB):
        g_t[:, i * QB : (i + 1) * QB] = nt(weight, g_all[2 * i : 2 * i + 2].reshape(QB, D)).astype(BF16)

    def queries_in(h):
        wait_bytes(came_q.at[h, 0 : N_DP - 1], slot_recv.at[1 + h])
        for c in range(4):
            two = nn(gather, slot_rows(came_q.at[h], slice(c * 256, (c + 1) * 256))).astype(BF16)
            packed_q[h, 2 * c] = two[:, :HEAD]
            packed_q[h, 2 * c + 1] = two[:, HEAD:]
        each_other(
            N_SEQ, s, lambda t: remote(packed_q.at[h, t], q_all.at[h, s], head_send.at[2 + h], head_recv.at[2 + h], t, d).start()
        )
        keep = pltpu.make_async_copy(packed_q.at[h, s], q_all.at[h, s], own.at[2 + h])
        keep.start()
        return keep

    def one_head(h):
        rows = slice(h * HEAD, (h + 1) * HEAD)
        for i in reversed(range(SEQ_LEN // QB)):
            first, last = 2 * max(0, i - 2), 2 * (i + 1)
            lo, hi = first * TOK, last * TOK
            here = slice(i * QB, hi)
            q_block = q_all[h, 2 * i : 2 * i + 2].reshape(QB, HEAD)
            k_block = k_all[first:last].reshape(hi - lo, HEAD)
            v_block = v_all[first:last].reshape(hi - lo, HEAD)
            keys = doc_c[lo:hi, :]
            same = jnp.concatenate([keys, keys], axis=1) == doc_row[:, here]
            earlier = lax.broadcasted_iota(jnp.int32, (hi - lo, QB), 0) + lo <= lax.broadcasted_iota(
                jnp.int32, (hi - lo, QB), 1
            ) + i * QB
            scores = jnp.where(same & earlier, nt(k_block, q_block) * SOFT_SCALE, NEG_FILL)
            terms = jnp.exp(scores - jnp.max(scores, axis=0, keepdims=True))
            weights = terms * (1.0 / jnp.sum(terms, axis=0, keepdims=True))
            weights_low = weights.astype(BF16)
            out = nn(v_t[:, lo:hi], weights_low).astype(BF16)
            o_t[rows, here] = out
            grad = g_t[rows, here]
            delta = jnp.sum(grad.astype(F32) * out.astype(F32), axis=0, keepdims=True)
            dscores = (weights * (nn(v_block, grad) - delta)).astype(BF16)
            dq_block = (nn(k_t[:, lo:hi], dscores) * SOFT_SCALE).T.astype(BF16)
            dq_all[h, 2 * i] = dq_block[:TOK]
            dq_all[h, 2 * i + 1] = dq_block[TOK:]
            dk_sum[lo:hi, :] += nn(dscores, q_block)
            dv_sum[lo:hi, :] += nt(weights_low, grad)
            to_owners(i, dq_all.at[h], back_q.at[h], h)
            if h == 1:
                dk_part[2 * i : 2 * i + 2] = (dk_sum[here, :] * SOFT_SCALE).astype(BF16).reshape(2, TOK, HEAD)
                dv_part[2 * i : 2 * i + 2] = dv_sum[here, :].astype(BF16).reshape(2, TOK, HEAD)
                to_owners(i, dk_part, back_k, 2)
                to_owners(i, dv_part, back_v, 3)

    def to_owners(i, src, dst, j):
        for t in (2 * i, 2 * i + 1):

            @pl.when(s != t)
            def _():
                remote(src.at[t], dst.at[s], back_send.at[j], back_recv.at[j], t, d).start()

    def keep_own(src, dst, j):
        keep = pltpu.make_async_copy(src.at[s], dst.at[s], own.at[4 + j])
        keep.start()
        return keep

    def arrived(keep, dst, j):
        keep.wait()
        wait_bytes(dst.at[0 : N_SEQ - 1], back_recv.at[j])

    def wo_half(h):
        part = slice(4 * h, 4 * h + 4)
        for c in range(D // 256):
            cols = slice(c * 256, (c + 1) * 256)
            product = nn(o_t[h * HEAD : (h + 1) * HEAD, :], g_all[:, :, cols].reshape(SEQ_LEN, 256))
            wo_part[part, :, :, cols] = product.reshape(4, N_X, PACK, 256).astype(BF16)
        each_other(
            N_X, x, lambda p: remote(wo_part.at[part, p], wo_x.at[x, part], wo_send.at[h], wo_recv.at[h], s, z * N_X + p).start()
        )
        keep = pltpu.make_async_copy(wo_part.at[part, x], wo_x.at[x, part], own.at[h])
        keep.start()
        return keep

    def wo_half_sum(h, keep):
        part = slice(4 * h, 4 * h + 4)
        keep.wait()
        wait_bytes(wo_x.at[0 : N_X - 1, part], wo_recv.at[h])
        for c in range(D // 256):
            cols = slice(c * 256, (c + 1) * 256)
            total = wo_x[0, part, :, cols].astype(F32)
            for j in range(1, N_X):
                total += wo_x[j, part, :, cols].astype(F32)
            wo_mid[part, :, cols] = total.astype(BF16)
        for zz in range(4 * h, 4 * h + 4):

            @pl.when(z != zz)
            def _():
                remote(wo_mid.at[zz], wo_z.at[z], wo_send.at[2], wo_recv.at[2], s, zz * N_X + x).start()

    def queries_back(h, keep):
        arrived(keep, back_q.at[h], h)
        for g in range(N_SEQ):
            out_q[h, :, :, g * HEAD : (g + 1) * HEAD] = as_slots(nn(scatter, back_q[h, g]))
        send_slots(out_q.at[h], ret_q.at[h], out_send.at[h], ret_recv.at[h], s, d)
        keep = pltpu.make_async_copy(out_q.at[h, d], ret_q.at[h, d], own.at[2 + h])
        keep.start()
        return keep

    keep_q0 = queries_in(0)
    keep_q0.wait()
    wait_bytes(q_all.at[0, 0 : N_SEQ - 1], head_recv.at[2])
    one_head(0)
    keep_back0 = keep_own(dq_all.at[0], back_q.at[0], 0)
    keep_wo0 = wo_half(0)
    keep_q1 = queries_in(1)
    keep_ret0 = queries_back(0, keep_back0)
    keep_q1.wait()
    wait_bytes(q_all.at[1, 0 : N_SEQ - 1], head_recv.at[3])
    one_head(1)
    keep_back1 = keep_own(dq_all.at[1], back_q.at[1], 1)
    keep_k = keep_own(dk_part, back_k, 2)
    keep_v = keep_own(dv_part, back_v, 3)
    wo_half_sum(0, keep_wo0)
    keep_wo1 = wo_half(1)
    keep_ret1 = queries_back(1, keep_back1)
    arrived(keep_k, back_k, 2)
    arrived(keep_v, back_v, 3)
    for part, ref in enumerate((back_k, back_v)):
        for c in range(4):
            both = (ref[2 * c].astype(F32) + ref[2 * c + 1].astype(F32)).astype(BF16)
            cols = slice(part * 512 + c * HEAD, part * 512 + (c + 1) * HEAD)
            out_kv[:, :, cols] = as_slots(nn(scatter, both))
    send_slots(out_kv, ret_kv, out_send.at[2], ret_recv.at[2], s, d)
    keep_kv = pltpu.make_async_copy(out_kv.at[d], ret_kv.at[d], own.at[4])
    keep_kv.start()
    wo_half_sum(1, keep_wo1)
    keep_mid = pltpu.make_async_copy(wo_mid.at[z], wo_z.at[z], own.at[5])
    keep_mid.start()

    column = lax.broadcasted_iota(jnp.int32, (TOK, N_DP * PACK), 0)
    target = rows_of(column // PACK, peer, lax.rem(column, PACK))
    pick = (lax.broadcasted_iota(jnp.int32, (TOK, N_DP * PACK), 1) == target).astype(F32).astype(BF16)
    for h, keep in enumerate((keep_ret0, keep_ret1)):
        keep.wait()
        wait_bytes(ret_q.at[h, 0 : N_DP - 1], ret_recv.at[h])
        for c in range(4):
            two = nn(pick, slot_rows(ret_q.at[h], slice(c * 256, (c + 1) * 256))).astype(BF16)
            for e in range(2):
                at = (2 * c + e) * 256 + h * HEAD
                dq_out[:, at : at + HEAD] = two[:, e * HEAD : (e + 1) * HEAD]
    keep_kv.wait()
    wait_bytes(ret_kv.at[0 : N_DP - 1], ret_recv.at[2])
    for part, ref in enumerate((dk_out, dv_out)):
        for c in range(2):
            at = part * 512 + c * 256
            ref[:, c * 256 : (c + 1) * 256] = nn(pick, slot_rows(ret_kv, slice(at, at + 256))).astype(BF16)
    keep_mid.wait()
    wait_bytes(wo_z.at[0 : N_Z - 1], wo_recv.at[2])
    total = wo_z[0].astype(F32)
    for j in range(1, N_Z):
        total += wo_z[j].astype(F32)
    wo_out[...] = total * GRAD_SCALE

    for copy in (g_up, g_down, g_mate, half_up, mate_down, half_down, mate_up, mate_across):
        copy.wait_send()
    wait_bytes(w_all.at[:, 0 : N_X - 1], w_send.at[1])
    wait_bytes(came_kv.at[0 : N_DP - 1], slot_send.at[0])
    wait_bytes(k_all.at[0 : N_SEQ - 1], head_send.at[0])
    wait_bytes(v_all.at[0 : N_SEQ - 1], head_send.at[1])
    wait_bytes(back_k.at[0 : N_SEQ - 1], back_send.at[2])
    wait_bytes(back_v.at[0 : N_SEQ - 1], back_send.at[3])
    wait_bytes(ret_kv.at[0 : N_DP - 1], out_send.at[2])
    wait_bytes(wo_z.at[0 : N_Z - 1], wo_send.at[2])
    for h in range(2):
        wait_bytes(came_q.at[h, 0 : N_DP - 1], slot_send.at[1 + h])
        wait_bytes(q_all.at[h, 0 : N_SEQ - 1], head_send.at[2 + h])
        wait_bytes(back_q.at[h, 0 : N_SEQ - 1], back_send.at[h])
        wait_bytes(ret_q.at[h, 0 : N_DP - 1], out_send.at[h])
        wait_bytes(wo_x.at[0 : N_X - 1, 4 * h : 4 * h + 4], wo_send.at[h])


def write_out(*refs):
    ins, outs, held, (came, gone) = refs[:4], refs[4:8], refs[8:12], refs[12:]
    for i in range(4):
        pltpu.make_async_copy(ins[i], held[i], came.at[i]).start()
    for i in range(4):
        pltpu.make_async_copy(ins[i], held[i], came.at[i]).wait()
        pltpu.make_async_copy(held[i], outs[i], gone.at[i]).start()
    for i in range(4):
        pltpu.make_async_copy(held[i], outs[i], gone.at[i]).wait()


def body(q_rows, key_rows, value_rows, pack_peer, pack_slot, doc_ids, grad_out, out_weight):
    def sds(shape, dtype=BF16):
        return jax.ShapeDtypeStruct(shape, dtype)

    def buf(*shape, dtype=BF16):
        return pltpu.VMEM(shape, dtype)

    slot = (N_DP, PACK)
    heads = (N_SEQ, TOK, HEAD)
    made = pl.pallas_call(
        kernel,
        name="attention_backward",
        out_shape=(sds((TOK, D)), sds((TOK, 512)), sds((TOK, 512)), sds((PACK, D), F32)),
        in_specs=[ANY] * 8,
        out_specs=(VMEM,) * 4,
        scratch_shapes=[
            pltpu.SMEM((16,), jnp.int32), pltpu.SMEM((16,), jnp.int32),
            buf(TOK, D), buf(TOK, 512), buf(TOK, 512), buf(1, SEQ_LEN, dtype=jnp.int32),
            buf(N_SEQ, TOK, D), buf(N_Z, N_X, PACK, D),
            buf(*slot, KV_COLS + TOK), buf(2, *slot, KV_COLS), buf(*slot, KV_COLS + TOK), buf(2, *slot, KV_COLS),
            buf(*heads), buf(2, *heads), buf(2, *heads), buf(*heads), buf(*heads),
            buf(2 * HEAD, SEQ_LEN), buf(2 * HEAD, SEQ_LEN), buf(HEAD, SEQ_LEN), buf(HEAD, SEQ_LEN),
            buf(SEQ_LEN, HEAD, dtype=F32), buf(SEQ_LEN, HEAD, dtype=F32), buf(SEQ_LEN, HEAD, dtype=F32),
            buf(2, *heads), buf(*heads), buf(*heads),
            buf(2, *heads), buf(*heads), buf(*heads),
            buf(2, *slot, KV_COLS), buf(*slot, KV_COLS), buf(2, *slot, KV_COLS), buf(*slot, KV_COLS),
            buf(N_Z, N_X, PACK, D), buf(N_X, N_Z, PACK, D), buf(N_Z, PACK, D), buf(N_Z, PACK, D),
            *(pltpu.SemaphoreType.DMA((n,)) for n in (8, 3, 3, 4, 4, 8, 8, 2, 2, 4, 4, 3, 3, 3, 3)),
        ],
        compiler_params=pltpu.CompilerParams(collective_id=0, has_side_effects=True, vmem_limit_bytes=60 << 20),
    )(q_rows, key_rows, value_rows, pack_peer, pack_slot, doc_ids, grad_out, out_weight)
    return pl.pallas_call(
        write_out,
        name="write_out",
        out_shape=tuple(sds(a.shape, a.dtype) for a in made),
        in_specs=[ANY] * 4,
        out_specs=(ANY,) * 4,
        scratch_shapes=[
            buf(TOK, D), buf(TOK, 512), buf(TOK, 512), buf(PACK, D, dtype=F32),
            pltpu.SemaphoreType.DMA((4,)), pltpu.SemaphoreType.DMA((4,)),
        ],
    )(*made)


def solution(mesh):
    return jax.shard_map(
        body,
        mesh=mesh,
        in_specs=(
            P(("seq", "dp"), None),
            P(("seq", "dp"), None),
            P(("seq", "dp"), None),
            P(("seq", "dp")),
            P(("seq", "dp")),
            P("dp", None),
            P("dp", "seq", None),
            P(("seq", "dp"), None),
        ),
        out_specs=(
            P(("seq", "dp"), None),
            P(("seq", "dp"), None),
            P(("seq", "dp"), None),
            P(("seq", "dp"), None),
        ),
        check_vma=False,
    )
```
